1024 devices in a mesh: dp: 32 (over x, y, core), head: 32 (over z).
Axes of the slice: x: 4, y: 4, z: 32, core: 2. Of those that a mesh axis runs over, the one named last changes fastest.
Arguments:
- text: bfloat16 [4096, 8192], P('dp'), may hold values from -6 to 6
- q_weight: bfloat16 [8192, 4096], P(None, 'head'), may hold values from -0.0625 to 0.0625
- q_gain: float32 [128], replicated, may hold values from 0.1 to 1.9
- enc_hidden: bfloat16 [8192, 1280], P(('dp', 'head')), may hold values from -100 to 100
- enc_branch: bfloat16 [8192, 1280], P(('dp', 'head')), may hold values from -6 to 6
- enc_gate: float32 [1], replicated, may hold values from 0.3 to 1.5
- enc_gain: float32 [1280], replicated, may hold values from 0.1 to 1.9
- enc_bias: float32 [1280], replicated, may hold values from -3 to 3
- proj_weight: bfloat16 [1280, 8192], P(None, 'head'), may hold values from -0.15625 to 0.15625
- proj_bias: float32 [8192], P('head'), may hold values from -3 to 3
- kv_weight: bfloat16 [8192, 1024], P('head'), may hold values from -0.0625 to 0.0625
- k_gain: float32 [128], replicated, may hold values from 0.1 to 1.9
- attn_gate: float32 [1], replicated, may hold values from 0.3 to 1.5
- o_weight: bfloat16 [4096, 8192], P(None, 'head'), may hold values from -0.09375 to 0.09375
- d_update: bfloat16 [4096, 8192], P('dp', 'head'), may hold values from -12 to 12
- tile_counts: int32 [32, 3], P('dp'), may hold values from 1 to 4, 8 in all within a row
- image_sample: int32 [32, 3], P('dp'), may hold values from 0 to 1, as said below
- text_lengths: int32 [32, 2], P('dp'), may hold values from 1 to 64, as said below
Outputs:
- attn: bfloat16 [4096, 4096], P('dp', 'head')
- d_text: bfloat16 [4096, 8192], P('dp', 'head')
- d_features: bfloat16 [8192, 1280], P(('dp', 'head'))
- d_q_gain: float32 [128], replicated
- d_k_gain: float32 [128], replicated
The draws below stay inside these ranges and needn't reach their ends.
Inputs may be any that keep to these rules, and one draw needn't show every extreme that they name: `image_sample`: every sample of a group has at least one image. `text_lengths`: in every group one sample uses all 64 slots.
All inputs are finite; a program needn't handle non-finite values.
Results may differ from the reference program's by a relative error of at most 0.034.
Values may be sent and summed in bfloat16 or wider, within the bound.
A program may use at most 32 MiB of HBM per device.

```python
import math
import jax
import jax.numpy as jnp
import numpy as np
from jax import lax

D = 8192
ENC = 1280
HD = 128
KVH = 4
TXT = 64
SAMP = 2
IMG = 3
TILES_GRP = 8
MAXT = 4
TILE = 32
HEADS = 32
DGROUPS = 32
GRP = 256
TXT_TOK = 4096
IMG_TOK = 8192


def draw_enc_hidden(key, part):
    key = jax.random.fold_in(key, 11)
    first, second, third = jax.random.split(key, 3)
    row_scale = jnp.exp(jax.random.uniform(first, (IMG_TOK, 1), jnp.float32) * math.log(10.0))
    col_scale = jnp.exp(jax.random.uniform(second, (1, ENC), jnp.float32) * math.log(10.0))
    base = jax.random.normal(third, (IMG_TOK, ENC), jnp.float32)
    return (jnp.clip(base, -4.0, 4.0) * row_scale * col_scale / 4.0).astype(jnp.bfloat16)


def draw_d_update(key, part):
    key = jax.random.fold_in(key, 23)
    first = jax.random.fold_in(key, 0)
    place = jnp.arange(TXT_TOK, dtype=jnp.float32) / max(TXT_TOK - 1, 1)
    row_scale = (1.0 + 2.0 * place) / 3.0
    base = jax.random.normal(first, (TXT_TOK, D), jnp.float32)
    return (jnp.clip(base, -4.0, 4.0) * row_scale[:, None]).astype(jnp.bfloat16)


def draw_image_sample(key, part):
    key = jax.random.fold_in(key, 31)
    first, second = jax.random.split(key)
    alone = jax.random.randint(first, (DGROUPS, 1), 0, IMG)
    single = jax.random.randint(second, (DGROUPS, 1), 0, SAMP)
    images = jnp.arange(IMG, dtype=jnp.int32)[None, :]
    return jnp.where(images == alone, single, 1 - single).astype(jnp.int32)


def draw_text_lengths(key, part):
    key = jax.random.fold_in(key, 41)
    first, second = jax.random.split(key)
    lengths = jax.random.randint(first, (DGROUPS, SAMP), 1, TXT + 1)
    filled = jax.random.randint(second, (DGROUPS, 1), 0, SAMP)
    samples = jnp.arange(SAMP, dtype=jnp.int32)[None, :]
    return jnp.where(samples == filled, TXT, lengths).astype(jnp.int32)


def block_levels(own_key, shape, cuts, low, high):
    loudness = 1.0
    for axis_at, parts in cuts:
        steps = jax.random.uniform(jax.random.fold_in(jax.random.fold_in(own_key, 6), axis_at), (parts,), jnp.float32, low / len(cuts), high / len(cuts))
        loudness = loudness * jnp.repeat(jnp.exp(steps), shape[axis_at] // parts).reshape((-1,) + (1,) * (len(shape) - 1 - axis_at))
    return loudness


def split_up(amount, total, most, skew):
    weights = [(1 << 20) // math.isqrt(rank ** skew) + 1 for rank in range(2, amount + 1)]
    rest, given = total - most - (amount - 1), [1] * (amount - 1)
    while rest > 0:
        movable = [i for i in range(amount - 1) if given[i] < most]
        whole, budget = sum([weights[i] for i in movable]), rest
        for i in movable:
            addition = min(most - given[i], max(1, budget * weights[i] // whole), rest)
            given[i] = given[i] + addition
            rest = rest - addition
    return np.array([most] + given)


def ragged_sizes(stream_key, count, total, most, lean):
    if count == 2:
        one = jax.random.randint(stream_key, (), max(1, total - most), min(most, total - 1) + 1)
        return jnp.stack([one, total - one])
    sizes = jnp.asarray(split_up(count, total, most, lean), jnp.int32)
    pairs = (count - 1) // 2
    source_of, taker = sizes[1:1 + 2 * pairs:2], sizes[2:2 + 2 * pairs:2]
    margin = jnp.minimum(source_of - 1, most - taker)
    passed = jax.random.randint(jax.random.fold_in(stream_key, 1), (pairs,), 0, 1 << 20) % (margin + 1)
    sizes = sizes.at[1:1 + 2 * pairs:2].set(source_of - passed).at[2:2 + 2 * pairs:2].set(taker + passed)
    return sizes[jax.random.permutation(jax.random.fold_in(stream_key, 2), count)]


def noise(stream_key, shape, scale, bound, cuts=(), kind=jnp.bfloat16):
    drawn = jax.random.normal(stream_key, shape, jnp.float32) * scale
    if len(cuts) > 0:
        drawn = block_levels(stream_key, shape, cuts, -0.22, 0.18) * drawn
    return jnp.clip(drawn, min=-bound, max=bound).astype(kind)


def setup_inputs(seed: int = 0) -> dict:
    seeds = jax.random.split(jax.random.key(seed), 19)
    return {
        "text": noise(seeds[0], (TXT_TOK, D), 1.0, 6.0, ((0, 32),)),
        "q_weight": noise(seeds[1], (D, HEADS * HD), D ** -0.5, 0.0625, ((1, 32),)),
        "q_gain": jnp.clip(1.0 + 0.18 * jax.random.normal(seeds[2], (HD,), jnp.float32), 0.1, 1.9),
        "enc_hidden": draw_enc_hidden(jax.random.fold_in(seeds[18], 71), 0),
        "enc_branch": noise(seeds[4], (IMG_TOK, ENC), 1.0, 6.0, ((0, 1024),)),
        "enc_gate": jnp.clip(jax.random.uniform(seeds[5], (1,), jnp.float32, 0.3, 1.5), 0.3, 1.5),
        "enc_gain": jnp.clip(1.0 + 0.18 * jax.random.normal(seeds[6], (ENC,), jnp.float32), 0.1, 1.9),
        "enc_bias": noise(seeds[7], (ENC,), 0.5, 3.0, (), jnp.float32),
        "proj_weight": noise(seeds[8], (ENC, D), ENC ** -0.5, 0.15625, ((1, 32),)),
        "proj_bias": noise(seeds[9], (D,), 0.5, 3.0, ((0, 32),), jnp.float32),
        "kv_weight": noise(seeds[10], (D, KVH * 2 * HD), D ** -0.5, 0.0625, ((0, 32),)),
        "k_gain": jnp.clip(1.0 + 0.18 * jax.random.normal(seeds[11], (HD,), jnp.float32), 0.1, 1.9),
        "attn_gate": jnp.clip(jax.random.uniform(seeds[12], (1,), jnp.float32, 0.3, 1.5), 0.3, 1.5),
        "o_weight": noise(seeds[13], (HEADS * HD, D), (HEADS * HD) ** -0.5, 0.09375, ((1, 32),)),
        "d_update": draw_d_update(jax.random.fold_in(seeds[18], 71), 0),
        "tile_counts": jax.vmap(lambda own: ragged_sizes(own, IMG, TILES_GRP, MAXT, 0))(jax.random.split(seeds[15], DGROUPS)).reshape((DGROUPS, IMG)).astype(jnp.int32),
        "image_sample": draw_image_sample(jax.random.fold_in(seeds[18], 71), 0),
        "text_lengths": draw_text_lengths(jax.random.fold_in(seeds[18], 71), 0),
    }


EPSILON = 1e-05

def group_masks(tiles, owners, lengths):
    ends = jnp.cumsum(tiles, dtype=jnp.int32) * TILE
    key_rows = jnp.arange(GRP, dtype=jnp.int32)
    image_index = lax.optimization_barrier(jnp.sum((key_rows[:, None] >= ends[None, :]).astype(jnp.int32), axis=1, dtype=jnp.int32))
    picked = image_index[:, None] == jnp.arange(IMG, dtype=jnp.int32)[None, :]
    key_sample = lax.optimization_barrier(jnp.sum(jnp.where(picked, owners[None, :], 0), axis=1, dtype=jnp.int32))
    slots = jnp.arange(SAMP * TXT, dtype=jnp.int32)
    sample = slots // TXT
    chosen = sample[:, None] == jnp.arange(SAMP, dtype=jnp.int32)[None, :]
    limit = lax.optimization_barrier(jnp.sum(jnp.where(chosen, lengths[None, :], 0), axis=1, dtype=jnp.int32))
    valid = (slots % TXT < limit).astype(jnp.float32)
    allowed = (sample[:, None] == key_sample[None, :]).astype(jnp.float32)
    return (allowed, valid)

def reference(text, q_weight, q_gain, enc_hidden, enc_branch, enc_gate, enc_gain, enc_bias, proj_weight, proj_bias, kv_weight, k_gain, attn_gate, o_weight, d_update, tile_counts, image_sample, text_lengths):
    scale = HD ** (-0.5)
    sharing = HEADS // KVH
    slots_grp = SAMP * TXT
    features = enc_hidden.astype(jnp.float32) + jnp.tanh(enc_gate[0]) * enc_branch.astype(jnp.float32)
    centered = features - lax.optimization_barrier(jnp.mean(features, axis=1, keepdims=True))
    inv_std = lax.rsqrt(lax.optimization_barrier(jnp.mean(centered * centered, axis=1, keepdims=True)) + EPSILON)
    unit_feat = centered * inv_std
    normed = (unit_feat * enc_gain + enc_bias).astype(jnp.bfloat16)
    proj_feat = (jnp.dot(normed, proj_weight, preferred_element_type=jnp.float32) + proj_bias).astype(jnp.bfloat16)
    projected = jnp.dot(proj_feat, kv_weight, preferred_element_type=jnp.float32).reshape(IMG_TOK, KVH, 2 * HD)
    key_pre = projected[:, :, :HD]
    inv_key = lax.rsqrt(lax.optimization_barrier(jnp.mean(key_pre * key_pre, axis=2, keepdims=True)) + EPSILON)
    key_unit = key_pre * inv_key
    kv_rows = jnp.concatenate([key_unit * k_gain, projected[:, :, HD:]], axis=2).astype(jnp.bfloat16)
    query_pre = jnp.dot(text, q_weight, preferred_element_type=jnp.float32).reshape(TXT_TOK, HEADS, HD)
    inv_query = lax.rsqrt(lax.optimization_barrier(jnp.mean(query_pre * query_pre, axis=2, keepdims=True)) + EPSILON)
    query_unit = query_pre * inv_query
    q_scaled = (query_unit * q_gain * scale).astype(jnp.bfloat16)
    attn_sum = jnp.tanh(attn_gate[0]) * jnp.dot(d_update, o_weight.T, preferred_element_type=jnp.float32)

    def one_group(items):
        query_grp, kv_grp, grad_grp, tiles, owners, lengths = items
        allowed, valid = group_masks(tiles, owners, lengths)
        spread = jnp.repeat(kv_grp, sharing, axis=1)
        keys = spread[:, :, :HD].astype(jnp.float32)
        values = spread[:, :, HD:].astype(jnp.float32)
        query_f = query_grp.astype(jnp.float32)
        scores = jnp.einsum('thd,rhd->htr', query_f, keys)
        weighted = jnp.exp(scores) * allowed[None]
        probs = weighted / lax.optimization_barrier(jnp.sum(weighted, axis=2, keepdims=True))
        probs_low = lax.optimization_barrier(probs.astype(jnp.bfloat16)).astype(jnp.float32)
        attn_grp = (jnp.einsum('htr,rhd->thd', probs_low, values) * valid[:, None, None]).astype(jnp.bfloat16)
        d_attn = (grad_grp.reshape(slots_grp, HEADS, HD) * valid[:, None, None]).astype(jnp.bfloat16)
        d_attn_f = lax.optimization_barrier(d_attn).astype(jnp.float32)
        d_probs = jnp.einsum('thd,rhd->htr', d_attn_f, values)
        delta = lax.optimization_barrier(jnp.sum(d_probs * probs, axis=2, keepdims=True))
        d_scores = lax.optimization_barrier((probs * (d_probs - delta)).astype(jnp.bfloat16)).astype(jnp.float32)
        d_q_scaled = jnp.einsum('htr,rhd->thd', d_scores, keys)
        d_keys = jnp.einsum('htr,thd->rhd', d_scores, query_f).astype(jnp.bfloat16)
        d_values = jnp.einsum('htr,thd->rhd', probs_low, d_attn_f).astype(jnp.bfloat16)
        return (attn_grp.reshape(slots_grp, HEADS * HD), d_q_scaled, jnp.concatenate([d_keys, d_values], axis=2))
    attn, d_q_scaled, kv_grads = lax.map(one_group, (q_scaled.reshape(DGROUPS, slots_grp, HEADS, HD), kv_rows.reshape(DGROUPS, GRP, KVH, 2 * HD), attn_sum.reshape(DGROUPS, slots_grp, HEADS * HD), tile_counts, image_sample, text_lengths))
    attn = attn.reshape(TXT_TOK, HEADS * HD)
    d_q_scaled = d_q_scaled.reshape(TXT_TOK, HEADS, HD)
    kv_sum = kv_grads.reshape(IMG_TOK, KVH, sharing, 2 * HD).astype(jnp.float32).sum(axis=2)
    d_q_gain = lax.optimization_barrier(jnp.sum(d_q_scaled * query_unit, axis=(0, 1))) * scale
    d_key_part = kv_sum[:, :, :HD]
    d_k_gain = lax.optimization_barrier(jnp.sum(d_key_part * key_unit, axis=(0, 1)))
    query_grad = d_q_scaled * q_gain * scale
    d_queries = (inv_query * (query_grad - query_unit * lax.optimization_barrier(jnp.mean(query_grad * query_unit, axis=2, keepdims=True)))).astype(jnp.bfloat16)
    weight_heads = q_weight.reshape(D, HEADS, HD)

    def add_head(total, head_index):
        term = jnp.dot(d_queries[:, head_index], weight_heads[:, head_index].T, preferred_element_type=jnp.float32).astype(jnp.bfloat16)
        return (total + lax.optimization_barrier(term).astype(jnp.float32), None)
    d_text, unused = lax.scan(add_head, jnp.zeros((TXT_TOK, D), jnp.float32), jnp.arange(HEADS, dtype=jnp.int32))
    key_grad = d_key_part * k_gain
    d_key_pre = inv_key * (key_grad - key_unit * lax.optimization_barrier(jnp.mean(key_grad * key_unit, axis=2, keepdims=True)))
    d_projected = jnp.concatenate([d_key_pre, kv_sum[:, :, HD:]], axis=2).reshape(IMG_TOK, KVH * 2 * HD).astype(jnp.bfloat16)
    d_proj_feat = jnp.dot(d_projected, kv_weight.T, preferred_element_type=jnp.float32).astype(jnp.bfloat16)
    d_normed = jnp.dot(d_proj_feat, proj_weight.T, preferred_element_type=jnp.float32)
    feat_grad = d_normed * enc_gain
    d_features = inv_std * (feat_grad - lax.optimization_barrier(jnp.mean(feat_grad, axis=1, keepdims=True)) - unit_feat * lax.optimization_barrier(jnp.mean(feat_grad * unit_feat, axis=1, keepdims=True)))
    return (attn, d_text.astype(jnp.bfloat16), d_features.astype(jnp.bfloat16), d_q_gain, d_k_gain)
```

```python
import jax
import jax.numpy as jnp
from jax import lax
from jax.experimental import pallas as pl
from jax.experimental.pallas import tpu as pltpu
from jax.sharding import PartitionSpec as P

N = 32
TXT = 64
TILE = 32
W = 128
ENC = 1280
HALF = 640
AUG = 1408
TILES = 22
EPSILON = 1e-05
MESH = pl.DeviceIdType.MESH
F32 = jnp.float32
BF16 = jnp.bfloat16

S_NRM, S_WRS, S_WAG, S_PLA, S_KV, S_KVG, S_DPA, S_FR, S_G1, S_G2, S_QT1, S_QT2, S_DQ = range(13)


def nn(a, b):
    return lax.dot_general(a, b, (((1,), (0,)), ((), ())), preferred_element_type=F32)


def nt(a, b):
    return lax.dot_general(a, b, (((1,), (1,)), ((), ())), preferred_element_type=F32)


def tn(a, b):
    return lax.dot_general(a, b, (((0,), (0,)), ((), ())), preferred_element_type=F32)


def kernel(
    tiles, owners, lengths, enc_gate, attn_gate,
    q_gain, k_gain, enc_hidden, enc_branch, enc_gain, enc_bias, proj_bias, d_update,
    text, q_weight, proj_weight, kv_weight, o_weight,
    attn_out, text_out, feat_out, qg_out, kg_out,
    text_v, qw_v, pw_v, kvw_v, ow_v,
    nrm, wt, wr, ws, wf, pp, pr, kvs, kvr, kgs, kgr, dps, dpr, fs, fr,
    gs, gr, gs2, gr2, c_right, c_left, dqa, qt,
    qu_v, qs_v, qi_v, ku_v, ki_v, unit_v, istd_v, acc,
    load_sem, send, recv, ring_send, ring_recv, dq_recv,
):
    dp = lax.axis_index("dp")
    z = lax.axis_index("head")

    def z_at(k):
        return lax.rem(z + k + 2 * N, N)

    def remote(src, dst, s_sem, r_sem, dev):
        return pltpu.make_async_remote_copy(
            src_ref=src, dst_ref=dst, send_sem=s_sem, recv_sem=r_sem,
            device_id=dev, device_id_type=MESH,
        )

    def wait_for(sem, ref):
        pltpu.make_async_copy(ref, ref, sem).wait()

    def far_first(n):
        step = (n + 1) // 2
        return jnp.where(lax.rem(n, 2) == 1, 16 + step, 16 - step)

    def to_z(stage, src_of, dst):
        def one(n, _):
            to = z_at(far_first(n))
            remote(src_of(to), dst, send.at[stage], recv.at[stage], (dp, to)).start()
            return 0
        lax.fori_loop(0, N - 1, one, 0)

    def to_plane(stage, src_of, dst):
        def one(n, _):
            to = lax.rem(dp + far_first(n), N)
            remote(src_of(to), dst, send.at[stage], recv.at[stage], (to, z)).start()
            return 0
        lax.fori_loop(0, N - 1, one, 0)

    loads = [
        pltpu.make_async_copy(src, dst, load_sem.at[n])
        for n, (src, dst) in enumerate((
            (proj_weight, pw_v), (kv_weight, kvw_v), (o_weight, ow_v),
            (q_weight, qw_v), (text, text_v),
        ))
    ]
    for load in loads:
        load.start()
    wf[...] = jnp.zeros_like(wf)

    barrier = pltpu.get_barrier_semaphore()

    def greet(k, _):
        pl.semaphore_signal(barrier, inc=1, device_id=(dp, z_at(k)), device_id_type=MESH)
        pl.semaphore_signal(
            barrier, inc=1, device_id=(lax.rem(dp + k, N), z), device_id_type=MESH
        )
        return 0

    lax.fori_loop(1, N, greet, 0)

    gate = jnp.tanh(jnp.full((8, ENC), enc_gate[0, 0], F32))
    features = enc_hidden[...].astype(F32) + gate * enc_branch[...].astype(F32)
    centered = features - jnp.mean(features, axis=1, keepdims=True)
    inv_std = lax.rsqrt(jnp.mean(centered * centered, axis=1, keepdims=True) + EPSILON)
    unit = centered * inv_std
    unit_v[...] = unit
    istd_v[...] = jnp.broadcast_to(inv_std, (8, W))
    normed = unit * enc_gain[...] + enc_bias[...]
    nrm[dp] = jnp.concatenate([normed[:, :HALF], normed[:, HALF:]], axis=0).astype(BF16)

    block = dp // 4
    quarter = lax.rem(dp, 4)
    rows0 = 32 * quarter
    loads[0].wait()
    loads[1].wait()
    kv_t = kvw_v[:, pl.ds(pl.multiple_of(W * block, W), W)].astype(F32).T.astype(BF16)
    wt[:, :ENC] = nt(kv_t, pw_v[...]).astype(BF16)
    first_row = lax.broadcasted_iota(jnp.int32, (W, 256), 0) == 0
    bias_rows = jnp.where(first_row, jnp.broadcast_to(proj_bias[...], (W, 256)), 0.0).astype(BF16)
    wt[:, ENC:] = nt(kv_t, bias_rows).astype(BF16)

    def tile_of(ref, t):
        row = pl.multiple_of(rows0 + 16 * (t // 11), 16)
        col = pl.multiple_of(W * lax.rem(t, 11), W)
        return ref.at[pl.ds(row, 16), pl.ds(col, W)]

    own_tile = (11 * z + 15) // 16
    owning = jnp.logical_and(own_tile < TILES, (16 * own_tile) // 11 == z)

    def term(d):
        return nt(d_update[...], ow_v[pl.ds(pl.multiple_of(W * d, W), W), :])

    loads[2].wait()
    c_right[0] = term(z_at(16)).astype(BF16)
    c_left[0] = term(z_at(-15)).astype(BF16)

    pl.semaphore_wait(barrier, 2 * (N - 1))

    def send_tile(n, _):
        t = lax.rem((11 * z_at(16) + 15) // 16 + n, TILES)
        to = (16 * t) // 11

        @pl.when(to != z)
        def _():
            remote(tile_of(wt, t), wr.at[z], send.at[S_WRS], recv.at[S_WRS], (dp, to)).start()
        return 0

    lax.fori_loop(0, TILES, send_tile, 0)

    def ring_copies(s):
        return (
            remote(c_right.at[s], c_right.at[s + 1], ring_send.at[0, s], ring_recv.at[0, s],
                   (dp, z_at(1))),
            remote(c_left.at[s], c_left.at[s + 1], ring_send.at[1, s], ring_recv.at[1, s],
                   (dp, z_at(-1))),
        )

    for copy in ring_copies(0):
        copy.start()
    to_plane(S_NRM, lambda to: nrm.at[dp], nrm.at[dp])

    def ring_steps(low, high):
        def one(s, _):
            own_right = term(z_at(16 - s))
            own_left = term(z_at(s - 15))
            before = ring_copies(s - 1)
            now = ring_copies(s)
            before[0].wait_recv()
            c_right[s] = (c_right[s].astype(F32) + own_right).astype(BF16)
            now[0].start()
            before[1].wait_recv()
            c_left[s] = (c_left[s].astype(F32) + own_left).astype(BF16)
            now[1].start()
            return 0
        lax.fori_loop(low, high, one, 0)

    loads[3].wait()
    loads[4].wait()
    query_pre = nn(text_v[...], qw_v[...])
    inv_query = lax.rsqrt(jnp.mean(query_pre * query_pre, axis=1, keepdims=True) + EPSILON)
    scale = W ** (-0.5)
    query_unit = query_pre * inv_query
    qu_v[...] = query_unit
    qi_v[...] = jnp.broadcast_to(inv_query, (W, W))
    qs_v[...] = (query_unit * q_gain[...] * scale).astype(BF16)

    ring_steps(1, 4)

    @pl.when(owning)
    def _():
        wait_for(recv.at[S_WRS], wr.at[pl.ds(0, N - 1)])
        wr[z] = tile_of(wt, own_tile)[...]
        tile = jnp.sum(wr[...].astype(F32), axis=0).astype(BF16)
        ws[...] = tile
        tile_of(wf, own_tile)[...] = tile
        to_z(S_WAG, lambda to: ws, tile_of(wf, own_tile))

    ring_steps(4, 8)

    @pl.when(owning)
    def _():
        wait_for(recv.at[S_WAG], wr.at[pl.ds(0, TILES - 1)])

    @pl.when(jnp.logical_not(owning))
    def _():
        wait_for(recv.at[S_WAG], wr.at[pl.ds(0, TILES)])

    wait_for(recv.at[S_NRM], nrm.at[pl.ds(0, N - 1)])

    plane = nrm[...].reshape(2 * 256, HALF)
    half_a = nt(plane, wf[:, :HALF]).reshape(N, 16, W)
    half_b = nt(plane, wf[:, HALF:ENC]).reshape(N, 16, W)
    ones = jnp.where(lax.broadcasted_iota(jnp.int32, (8, W), 1) == 0, 1.0, 0.0).astype(BF16)
    bias = nt(ones, wf[:, ENC:])
    pp[...] = half_a[:, :8] + half_b[:, 8:] + bias[None]
    to_plane(S_PLA, lambda to: pp.at[to], pr.at[dp])
    pr[dp] = pp[dp]

    chip = dp // 2
    core = lax.rem(dp, 2)
    part = pl.ds(pl.multiple_of(16 * chip, 16), 16)
    even = lax.rem(z, 2) == core

    @pl.when(even)
    def _():
        to_z(
            S_QT1,
            lambda to: qw_v.at[pl.ds(pl.multiple_of(256 * to + 16 * chip, 16), 16)],
            qt.at[core, z // 2, part],
        )
        qt[core, z // 2, part] = qw_v[pl.ds(pl.multiple_of(256 * z + 16 * chip, 16), 16)]

    ring_steps(8, 10)

    wait_for(recv.at[S_PLA], pr.at[pl.ds(0, N - 1)])
    blocks = jnp.sum(pr[...].reshape(8, 4, 8, W), axis=1)
    for k in range(4):
        key_pre = blocks[2 * k]
        inv_key = lax.rsqrt(jnp.mean(key_pre * key_pre, axis=1, keepdims=True) + EPSILON)
        key_unit = key_pre * inv_key
        ku_v[k] = key_unit
        ki_v[k] = jnp.broadcast_to(inv_key, (8, W))
        kvs[k] = jnp.concatenate([key_unit * k_gain[...], blocks[2 * k + 1]], axis=0).astype(BF16)
    to_z(S_KV, lambda to: kvs.at[to // 8], kvr.at[z])
    kvr[z] = kvs[z // 8]

    ring_steps(10, 13)

    @pl.when(even)
    def _():
        wait_for(recv.at[S_QT1], kvr.at[pl.ds(0, 15)])

    @pl.when(jnp.logical_not(even))
    def _():
        wait_for(recv.at[S_QT1], kvr.at[pl.ds(0, 16)])

    to_plane(S_QT2, lambda to: qt.at[core, :, part], qt.at[core, :, part])

    ring_steps(13, 15)
    own_right = term(z_at(1))
    before = ring_copies(14)
    before[0].wait_recv()
    c_right[15] = (c_right[15].astype(F32) + own_right).astype(BF16)
    last = ring_copies(15)[0]
    last.start()

    wait_for(recv.at[S_KV], kvr.at[pl.ds(0, N - 1)])
    kv_f = kvr[...].astype(F32)
    keys = kv_f[:, :8].reshape(256, W).astype(BF16)
    values = kv_f[:, 8:].reshape(256, W).astype(BF16)
    row = lax.broadcasted_iota(jnp.int32, (W, 256), 1)
    slot = lax.broadcasted_iota(jnp.int32, (W, 256), 0)
    end0 = tiles[0, 0] * TILE
    end1 = end0 + tiles[0, 1] * TILE
    key_sample = jnp.where(
        row < end0, owners[0, 0], jnp.where(row < end1, owners[0, 1], owners[0, 2])
    )
    allowed = jnp.where((slot >= TXT).astype(jnp.int32) == key_sample, 1.0, 0.0)
    slot_w = lax.broadcasted_iota(jnp.int32, (W, W), 0)
    limit = jnp.where(slot_w >= TXT, lengths[0, 1] + TXT, lengths[0, 0])
    valid = jnp.where(slot_w < limit, 1.0, 0.0)
    q_scaled = qs_v[...]
    weighted = jnp.exp(nt(q_scaled, keys)) * allowed
    probs = weighted / jnp.sum(weighted, axis=1, keepdims=True)
    probs_low = probs.astype(BF16)
    attn_out[...] = (nn(probs_low, values) * valid).astype(BF16)

    before[1].wait_recv()
    own = term(z) + c_left[15].astype(F32)
    last.wait_recv()
    attn_total = c_right[16].astype(F32) + own
    d_gate = jnp.tanh(jnp.full((W, W), attn_gate[0, 0], F32))
    d_attn = (d_gate * attn_total * valid).astype(BF16)
    d_probs = nt(d_attn, values)
    delta = jnp.sum(d_probs * probs, axis=1, keepdims=True)
    d_scores_f = probs * (d_probs - delta)
    d_q_scaled = nn(d_scores_f.astype(BF16), keys)
    query_unit = qu_v[...]
    grad = d_q_scaled * q_gain[...] * scale
    d_queries = qi_v[...] * (grad - query_unit * jnp.mean(grad * query_unit, axis=1, keepdims=True))
    dqa[z] = d_queries.astype(BF16)

    def pass_on(from_z, hops):
        remote(dqa.at[from_z], dqa.at[from_z], send.at[S_DQ], dq_recv.at[from_z],
               (dp, z_at(hops))).start()

    def arrived(from_z):
        remote(dqa.at[from_z], dqa.at[from_z], send.at[S_DQ], dq_recv.at[from_z],
               (dp, z_at(1))).wait_recv()

    for hops in (4, -4, 2, -2, 1, -1):
        pass_on(z, hops)

    d_scores = d_scores_f.astype(BF16).astype(F32).T.astype(BF16)
    probs_t = probs_low.astype(F32).T.astype(BF16)
    d_keys = nn(d_scores, q_scaled)
    d_values = nn(probs_t, d_attn)
    kgs[...] = jnp.concatenate(
        [d_keys.reshape(N, 8, W), d_values.reshape(N, 8, W)], axis=1
    ).astype(BF16)
    to_z(S_KVG, lambda to: kgs.at[to], kgr.at[z])
    kgr[z] = kgs[z]
    query_part = jnp.sum(d_q_scaled * query_unit, axis=0, keepdims=True) * scale

    wait_for(recv.at[S_QT2], qw_v.at[pl.ds(0, 7936)])

    def text_term(head):
        return nt(dqa[head], qt[lax.rem(head, 2), head // 2])

    acc[...] = text_term(z)

    def relay(k):
        for sign in (1, -1):
            near = z_at(-sign * (4 * k + 2))
            arrived(near)
            pass_on(near, sign)
        for sign in (1, -1):
            if k == 3 and sign == -1:
                continue
            far = z_at(-sign * (4 * k + 4))
            arrived(far)
            if k < 3:
                if not (k == 2 and sign == -1):
                    pass_on(far, 4 * sign)
                pass_on(far, 2 * sign)
                pass_on(far, sign)

    def use(k):
        total = acc[...]
        for j in (2, 4):
            for sign in (1, -1):
                if k == 3 and j == 4 and sign == -1:
                    continue
                total = total + text_term(z_at(-sign * (4 * k + j)))
        for j in (1, 3):
            for sign in (1, -1):
                from_z = z_at(-sign * (4 * k + j))
                arrived(from_z)
                total = total + text_term(from_z)
        acc[...] = total

    relay(0)
    relay(1)
    use(0)

    wait_for(recv.at[S_KVG], kgr.at[pl.ds(0, N - 1)])
    kv_sum = jnp.sum(kgr[...].astype(F32).reshape(4, 8, 16, W), axis=1)
    key_part = jnp.zeros((8, W), F32)
    for k in range(4):
        d_key = kv_sum[k, :8]
        key_unit = ku_v[k]
        key_part = key_part + d_key * key_unit
        key_grad = d_key * k_gain[...]
        dps[2 * k] = ki_v[k] * (
            key_grad - key_unit * jnp.mean(key_grad * key_unit, axis=1, keepdims=True)
        )
        dps[2 * k + 1] = kv_sum[k, 8:]
    to_plane(S_DPA, lambda to: dps.at[to // 4], dpr.at[dp])
    dpr[dp] = dps[dp // 4]
    key_part = jnp.sum(key_part, axis=0, keepdims=True)
    row8 = lax.broadcasted_iota(jnp.int32, (8, W), 0)
    gs[...] = jnp.where(
        row8 == 0, jnp.broadcast_to(query_part, (8, W)), jnp.broadcast_to(key_part, (8, W))
    )
    to_plane(S_G1, lambda to: gs, gr.at[dp])
    gr[dp] = gs[...]

    relay(2)
    use(1)

    wait_for(recv.at[S_DPA], dpr.at[pl.ds(0, N - 1)])
    d_plane = nn(dpr[...].reshape(256, W).astype(BF16), wf[:, :ENC])
    fs[...] = jnp.concatenate(
        [d_plane[:, :HALF].reshape(N, 8, HALF), d_plane[:, HALF:].reshape(N, 8, HALF)], axis=1
    ).astype(BF16)
    to_plane(S_FR, lambda to: fs.at[to], fr.at[dp])
    fr[dp] = fs[dp]

    wait_for(recv.at[S_G1], gr.at[pl.ds(0, N - 1)])
    gs2[...] = jnp.sum(gr[...], axis=0)
    to_z(S_G2, lambda to: gs2, gr2.at[z])
    gr2[z] = gs2[...]

    relay(3)
    use(2)

    wait_for(recv.at[S_FR], fr.at[pl.ds(0, N - 1)])
    back = jnp.sum(fr[...].astype(F32), axis=0)
    d_normed = jnp.concatenate([back[:8], back[8:]], axis=1)
    feat_grad = d_normed * enc_gain[...]
    unit = unit_v[...]
    feat_out[...] = (
        istd_v[:, :1]
        * (
            feat_grad
            - jnp.mean(feat_grad, axis=1, keepdims=True)
            - unit * jnp.mean(feat_grad * unit, axis=1, keepdims=True)
        )
    ).astype(BF16)

    use(3)
    text_out[...] = acc[...].astype(BF16)

    wait_for(recv.at[S_G2], gr2.at[pl.ds(0, N - 1)])
    gains = jnp.sum(gr2[...], axis=0)
    qg_out[...] = gains[0:1]
    kg_out[...] = gains[1:2]

    for s in range(16):
        copies = ring_copies(s)
        copies[0].wait_send()
        if s < 15:
            copies[1].wait_send()
    wait_for(send.at[S_NRM], nrm.at[pl.ds(0, N - 1)])
    wait_for(send.at[S_PLA], pp.at[pl.ds(0, N - 1)])
    wait_for(send.at[S_KV], kvr.at[pl.ds(0, N - 1)])
    wait_for(send.at[S_KVG], kgr.at[pl.ds(0, N - 1)])
    wait_for(send.at[S_DPA], dpr.at[pl.ds(0, N - 1)])
    wait_for(send.at[S_FR], fr.at[pl.ds(0, N - 1)])
    wait_for(send.at[S_G1], gr.at[pl.ds(0, N - 1)])
    wait_for(send.at[S_G2], gr2.at[pl.ds(0, N - 1)])
    wait_for(send.at[S_QT2], qw_v.at[pl.ds(0, 7936)])
    wait_for(send.at[S_DQ], dqa.at[pl.ds(0, N - 1)])

    @pl.when(owning)
    def _():
        wait_for(send.at[S_WRS], wr.at[pl.ds(0, TILES - 1)])
        wait_for(send.at[S_WAG], wr.at[pl.ds(0, N - 1)])

    @pl.when(jnp.logical_not(owning))
    def _():
        wait_for(send.at[S_WRS], wr.at[pl.ds(0, TILES)])

    @pl.when(even)
    def _():
        wait_for(send.at[S_QT1], kvr.at[pl.ds(0, N - 1)])


def on_device(
    text, q_weight, q_gain, enc_hidden, enc_branch, enc_gate, enc_gain, enc_bias,
    proj_weight, proj_bias, kv_weight, k_gain, attn_gate, o_weight, d_update,
    tile_counts, image_sample, text_lengths,
):
    vmem = pl.BlockSpec(memory_space=pltpu.VMEM)
    smem = pl.BlockSpec(memory_space=pltpu.SMEM)
    anywhere = pl.BlockSpec(memory_space=pl.ANY)
    scratch = [
        pltpu.VMEM((128, 8192), BF16), pltpu.VMEM((8192, W), BF16),
        pltpu.VMEM((ENC, 256), BF16), pltpu.VMEM((256, 1024), BF16),
        pltpu.VMEM((4096, 256), BF16),
        pltpu.VMEM((N, 16, HALF), BF16),
        pltpu.VMEM((W, AUG), BF16),
        pltpu.VMEM((N, 16, W), BF16),
        pltpu.VMEM((16, W), BF16),
        pltpu.VMEM((W, AUG), BF16),
        pltpu.VMEM((N, 8, W), F32), pltpu.VMEM((N, 8, W), F32),
        pltpu.VMEM((4, 16, W), BF16), pltpu.VMEM((N, 16, W), BF16),
        pltpu.VMEM((N, 16, W), BF16), pltpu.VMEM((N, 16, W), BF16),
        pltpu.VMEM((8, 8, W), F32), pltpu.VMEM((N, 8, W), F32),
        pltpu.VMEM((N, 16, HALF), BF16), pltpu.VMEM((N, 16, HALF), BF16),
        pltpu.VMEM((8, W), F32), pltpu.VMEM((N, 8, W), F32),
        pltpu.VMEM((8, W), F32), pltpu.VMEM((N, 8, W), F32),
        pltpu.VMEM((17, W, W), BF16), pltpu.VMEM((17, W, W), BF16),
        pltpu.VMEM((N, W, W), BF16),
        pltpu.VMEM((2, 16, 256, W), BF16),
        pltpu.VMEM((W, W), F32), pltpu.VMEM((W, W), BF16), pltpu.VMEM((W, W), F32),
        pltpu.VMEM((4, 8, W), F32), pltpu.VMEM((4, 8, W), F32),
        pltpu.VMEM((8, ENC), F32), pltpu.VMEM((8, W), F32),
        pltpu.VMEM((W, 256), F32),
        pltpu.SemaphoreType.DMA((5,)),
        pltpu.SemaphoreType.DMA((13,)), pltpu.SemaphoreType.DMA((13,)),
        pltpu.SemaphoreType.DMA((2, 16)), pltpu.SemaphoreType.DMA((2, 16)),
        pltpu.SemaphoreType.DMA((N,)),
    ]
    attn, d_text, d_features, d_q_gain, d_k_gain = pl.pallas_call(
        kernel,
        out_shape=(
            jax.ShapeDtypeStruct((128, W), BF16),
            jax.ShapeDtypeStruct((128, 256), BF16),
            jax.ShapeDtypeStruct((8, ENC), BF16),
            jax.ShapeDtypeStruct((1, W), F32),
            jax.ShapeDtypeStruct((1, W), F32),
        ),
        in_specs=[smem] * 5 + [vmem] * 8 + [anywhere] * 5,
        out_specs=(vmem,) * 5,
        scratch_shapes=scratch,
        compiler_params=pltpu.CompilerParams(
            collective_id=0, has_side_effects=True, vmem_limit_bytes=40 << 20
        ),
        name="layer",
    )(
        tile_counts, image_sample, text_lengths, enc_gate.reshape(1, 1), attn_gate.reshape(1, 1),
        q_gain.reshape(1, W), k_gain.reshape(1, W), enc_hidden, enc_branch,
        enc_gain.reshape(1, ENC), enc_bias.reshape(1, ENC), proj_bias.reshape(1, 256), d_update,
        text, q_weight, proj_weight, kv_weight, o_weight,
    )
    return attn, d_text, d_features, d_q_gain.reshape(W), d_k_gain.reshape(W)


def solution(mesh):
    in_specs = (
        P("dp", None),
        P(None, "head"),
        P(),
        P(("dp", "head"), None),
        P(("dp", "head"), None),
        P(),
        P(),
        P(),
        P(None, "head"),
        P("head"),
        P("head", None),
        P(),
        P(),
        P(None, "head"),
        P("dp", "head"),
        P("dp", None),
        P("dp", None),
        P("dp", None),
    )
    out_specs = (P("dp", "head"), P("dp", "head"), P(("dp", "head"), None), P(), P())
    return jax.shard_map(
        on_device, mesh=mesh, in_specs=in_specs, out_specs=out_specs, check_vma=False
    )
```

```python
import jax
import jax.numpy as jnp
from jax import lax
from jax.experimental import pallas as pl
from jax.experimental.pallas import tpu as pltpu
from jax.sharding import PartitionSpec as P

N = 32
TXT = 64
TILE = 32
W = 128
ENC = 1280
HALF = 640
AUG = 1408
TILES = 22
EPSILON = 1e-05
MESH = pl.DeviceIdType.MESH
F32 = jnp.float32
BF16 = jnp.bfloat16

(
    S_NRM, S_WRS, S_WAG, S_PLA, S_KV, S_KG1, S_KG2, S_G1, S_G2, S_QT1, S_QT2, S_QT3, S_WG1, S_WG2, S_DQ, S_C,
) = range(16)


def nn(a, b):
    return lax.dot_general(a, b, (((1,), (0,)), ((), ())), preferred_element_type=F32)


def nt(a, b):
    return lax.dot_general(a, b, (((1,), (1,)), ((), ())), preferred_element_type=F32)


def tn(a, b):
    return lax.dot_general(a, b, (((0,), (0,)), ((), ())), preferred_element_type=F32)


def kernel(
    enc_hidden_h, enc_branch_h, enc_gate_h, enc_gain_h, enc_bias_h, proj_weight, kv_weight, proj_bias_h,
    d_update_h, o_weight, tiles_h, owners_h, lengths_h, attn_gate_h, q_gain_h, k_gain_h,
    q_weight, text,
    attn_out, text_out, feat_out, qg_out, kg_out,
    enc_hidden, enc_branch, enc_gate, enc_gain, enc_bias, pw_v, kvw_v, proj_bias,
    d_update, ow_v, tiles, owners, lengths, attn_gate, q_gain, k_gain, qw_v, text_v,
    nrm, wt, wr, ws, wf, wg, pp, pr, kvs, kvr, kgs, kg1, kg2, kgr,
    gs, gr, gs2, gr2, terms, rx1, rx2, dqa, qt,
    qu_v, qs_v, qi_v, ku_v, ki_v, unit_v, istd_v, acc,
    load_sem, send, recv, c1_recv, c2_recv, dq_recv,
):
    dp = lax.axis_index("dp")
    z = lax.axis_index("head")

    def z_at(k):
        return lax.rem(z + k + 2 * N, N)

    def remote(src, dst, s_sem, r_sem, dev):
        return pltpu.make_async_remote_copy(
            src_ref=src, dst_ref=dst, send_sem=s_sem, recv_sem=r_sem,
            device_id=dev, device_id_type=MESH,
        )

    def wait_for(sem, ref):
        pltpu.make_async_copy(ref, ref, sem).wait()

    def far_first(n):
        step = (n + 1) // 2
        return jnp.where(lax.rem(n, 2) == 1, 16 + step, 16 - step)

    def to_z(stage, src_of, dst):
        def one(n, _):
            to = z_at(far_first(n))
            remote(src_of(to), dst, send.at[stage], recv.at[stage], (dp, to)).start()
            return 0
        lax.fori_loop(0, N - 1, one, 0)

    def to_plane(stage, src_of, dst):
        def one(n, _):
            to = lax.rem(dp + far_first(n), N)
            remote(src_of(to), dst, send.at[stage], recv.at[stage], (to, z)).start()
            return 0
        lax.fori_loop(0, N - 1, one, 0)

    loads = [
        pltpu.make_async_copy(src, dst, load_sem.at[n])
        for n, (src, dst) in enumerate((
            (kv_weight, kvw_v), (proj_weight, pw_v), (proj_bias_h, proj_bias),
            (enc_hidden_h, enc_hidden), (enc_branch_h, enc_branch), (enc_gate_h, enc_gate),
            (enc_gain_h, enc_gain), (enc_bias_h, enc_bias), (d_update_h, d_update),
            (o_weight, ow_v), (tiles_h, tiles), (owners_h, owners), (lengths_h, lengths),
            (attn_gate_h, attn_gate), (q_gain_h, q_gain), (k_gain_h, k_gain),
            (q_weight, qw_v), (text, text_v),
        ))
    ]
    for load in loads:
        load.start()
    wf[...] = jnp.zeros_like(wf)

    barrier = pltpu.get_barrier_semaphore()

    def greet(k, _):
        pl.semaphore_signal(barrier, inc=1, device_id=(dp, z_at(k)), device_id_type=MESH)
        pl.semaphore_signal(
            barrier, inc=1, device_id=(lax.rem(dp + k, N), z), device_id_type=MESH
        )
        return 0

    lax.fori_loop(1, N, greet, 0)

    block = dp // 4
    quarter = lax.rem(dp, 4)
    rows0 = 32 * quarter
    for load in loads[:3]:
        load.wait()
    kv_t = kvw_v[:, pl.ds(pl.multiple_of(W * block, W), W)].astype(F32).T.astype(BF16)
    wt[:, :ENC] = nt(kv_t, pw_v[...]).astype(BF16)
    first_row = lax.broadcasted_iota(jnp.int32, (W, 256), 0) == 0
    bias_rows = jnp.where(first_row, jnp.broadcast_to(proj_bias[...], (W, 256)), 0.0).astype(BF16)
    wt[:, ENC:] = nt(kv_t, bias_rows).astype(BF16)

    def tile_of(ref, t):
        row = pl.multiple_of(rows0 + 16 * (t // 11), 16)
        col = pl.multiple_of(W * lax.rem(t, 11), W)
        return ref.at[pl.ds(row, 16), pl.ds(col, W)]

    own_tile = (11 * z + 15) // 16
    owning = jnp.logical_and(own_tile < TILES, (16 * own_tile) // 11 == z)

    pl.semaphore_wait(barrier, 2 * (N - 1))

    def send_tile(n, _):
        t = lax.rem((11 * z_at(16) + 15) // 16 + n, TILES)
        to = (16 * t) // 11

        @pl.when(to != z)
        def _():
            remote(tile_of(wt, t), wr.at[z], send.at[S_WRS], recv.at[S_WRS], (dp, to)).start()
        return 0

    lax.fori_loop(0, TILES, send_tile, 0)

    for load in loads[3:8]:
        load.wait()
    gate = jnp.tanh(enc_gate[...])
    gain_row = jnp.concatenate([enc_gain[n : n + 1] for n in range(10)], axis=1)
    bias_row = jnp.concatenate([enc_bias[n : n + 1] for n in range(10)], axis=1)
    features = enc_hidden[...].astype(F32) + gate * enc_branch[...].astype(F32)
    centered = features - jnp.mean(features, axis=1, keepdims=True)
    inv_std = lax.rsqrt(jnp.mean(centered * centered, axis=1, keepdims=True) + EPSILON)
    unit = centered * inv_std
    unit_v[...] = unit
    istd_v[...] = jnp.broadcast_to(inv_std, (8, W))
    normed = unit * gain_row + bias_row
    nrm[dp] = jnp.concatenate([normed[:, :HALF], normed[:, HALF:]], axis=0).astype(BF16)

    to_plane(S_NRM, lambda to: nrm.at[dp], nrm.at[dp])

    for load in loads[8:10]:
        load.wait()
    for n in range(4):
        heads = nt(d_update[...], ow_v[1024 * n : 1024 * (n + 1)]).astype(BF16)
        for j in range(8):
            terms[8 * n + j] = heads[:, W * j : W * (j + 1)]

    sides = ((0, 1), (1, -1))

    def first_terms():
        remote(terms.at[z_at(16)], rx2.at[0, 7], send.at[S_C], c2_recv.at[0, 7],
               (dp, z_at(2))).start()

        def one(n, _):
            j = 7 - n
            for side, sign in sides:
                remote(terms.at[z_at(sign * (2 * j + 1))], rx1.at[side, j], send.at[S_C],
                       c1_recv.at[side, j], (dp, z_at(sign))).start()
            return 0
        lax.fori_loop(0, 8, one, 0)

    def reached(side, j, long):
        remote(terms.at[z], rx1.at[side, j], send.at[S_C], c1_recv.at[side, j],
               (dp, z_at(1))).wait_recv()
        total = rx1[side, j].astype(F32)
        if long:
            remote(terms.at[z], rx2.at[side, j], send.at[S_C], c2_recv.at[side, j],
                   (dp, z_at(1))).wait_recv()
            total = total + rx2[side, j].astype(F32)
        return total

    def send_on(side, sign, j, long):
        at = z_at(sign * 2 * j)
        terms[at] = (terms[at].astype(F32) + reached(side, j, long)).astype(BF16)
        remote(terms.at[at], rx2.at[side, j - 1], send.at[S_C], c2_recv.at[side, j - 1],
               (dp, z_at(2 * sign))).start()

    def next_terms(high, low):
        def one(n, _):
            for side, sign in sides:
                send_on(side, sign, high - n, True)
            return 0
        lax.fori_loop(0, high - low + 1, one, 0)

    chip = dp // 2
    core = lax.rem(dp, 2)

    def to_chips(stage, src, dst):
        def one(n, _):
            to = lax.rem(dp + 2 * n, N)
            remote(src, dst, send.at[stage], recv.at[stage], (to, z)).start()
            return 0
        lax.fori_loop(1, 16, one, 0)

    def to_sibling(stage, ref):
        remote(ref, ref, send.at[stage], recv.at[stage], (dp + 1 - 2 * core, z)).start()

    first_terms()

    for load in loads[10:]:
        load.wait()
    query_pre = nn(text_v[...], qw_v[...])
    inv_query = lax.rsqrt(jnp.mean(query_pre * query_pre, axis=1, keepdims=True) + EPSILON)
    scale = W ** (-0.5)
    query_unit = query_pre * inv_query
    qu_v[...] = query_unit
    qi_v[...] = jnp.broadcast_to(inv_query, (W, W))
    qs_v[...] = (query_unit * q_gain[...] * scale).astype(BF16)

    send_on(1, -1, 7, False)
    send_on(0, 1, 7, True)
    next_terms(6, 6)

    @pl.when(owning)
    def _():
        wait_for(recv.at[S_WRS], wr.at[pl.ds(0, N - 1)])
        wr[z] = tile_of(wt, own_tile)[...]
        tile = jnp.sum(wr[...].astype(F32), axis=0).astype(BF16)
        ws[...] = tile
        tile_of(wf, own_tile)[...] = tile
        to_z(S_WAG, lambda to: ws, tile_of(wf, own_tile))

    part = pl.ds(pl.multiple_of(16 * chip, 16), 16)
    even = lax.rem(z, 2) == core

    @pl.when(even)
    def _():
        to_z(
            S_QT1,
            lambda to: qw_v.at[pl.ds(pl.multiple_of(256 * to + 16 * chip, 16), 16)],
            qt.at[core, z // 2, part],
        )
        qt[core, z // 2, part] = qw_v[pl.ds(pl.multiple_of(256 * z + 16 * chip, 16), 16)]

    next_terms(5, 3)

    @pl.when(owning)
    def _():
        wait_for(recv.at[S_WAG], wr.at[pl.ds(0, TILES - 1)])

    @pl.when(jnp.logical_not(owning))
    def _():
        wait_for(recv.at[S_WAG], wr.at[pl.ds(0, TILES)])

    wait_for(recv.at[S_NRM], nrm.at[pl.ds(0, N - 1)])

    plane = nrm[...].reshape(2 * 256, HALF)
    half_a = nt(plane, wf[:, :HALF]).reshape(N, 16, W)
    half_b = nt(plane, wf[:, HALF:ENC]).reshape(N, 16, W)
    ones = jnp.where(lax.broadcasted_iota(jnp.int32, (8, W), 1) == 0, 1.0, 0.0).astype(BF16)
    bias = nt(ones, wf[:, ENC:])
    pp[...] = half_a[:, :8] + half_b[:, 8:] + bias[None]
    to_plane(S_PLA, lambda to: pp.at[to], pr.at[dp])
    pr[dp] = pp[dp]

    own_rows = wf.at[pl.ds(pl.multiple_of(rows0, 32), 32), pl.ds(0, ENC)]
    wg[chip, core] = own_rows[...]

    @pl.when(even)
    def _():
        wait_for(recv.at[S_QT1], kvr.at[pl.ds(0, 15)])

    @pl.when(jnp.logical_not(even))
    def _():
        wait_for(recv.at[S_QT1], kvr.at[pl.ds(0, 16)])

    to_chips(S_QT2, qt.at[core, :, part], qt.at[core, :, part])


    next_terms(2, 2)

    wait_for(recv.at[S_PLA], pr.at[pl.ds(0, N - 1)])
    blocks = jnp.sum(pr[...].reshape(8, 4, 8, W), axis=1)
    for k in range(4):
        key_pre = blocks[2 * k]
        inv_key = lax.rsqrt(jnp.mean(key_pre * key_pre, axis=1, keepdims=True) + EPSILON)
        key_unit = key_pre * inv_key
        ku_v[k] = key_unit
        ki_v[k] = jnp.broadcast_to(inv_key, (8, W))
        kvs[k] = jnp.concatenate([key_unit * k_gain[...], blocks[2 * k + 1]], axis=0).astype(BF16)
    to_z(S_KV, lambda to: kvs.at[to // 8], kvr.at[z])
    kvr[z] = kvs[z // 8]
    to_chips(S_WG1, wg.at[chip, core], wg.at[chip, core])

    next_terms(1, 1)

    row = lax.broadcasted_iota(jnp.int32, (W, 256), 1)
    slot = lax.broadcasted_iota(jnp.int32, (W, 256), 0)
    end0 = tiles[:, 0:1] * TILE
    end1 = end0 + tiles[:, 1:2] * TILE
    key_sample = jnp.where(
        row < end0, owners[:, 0:1], jnp.where(row < end1, owners[:, 1:2], owners[:, 2:3])
    )
    allowed = jnp.where((slot >= TXT).astype(jnp.int32) == key_sample, 1.0, 0.0)
    slot_w = lax.broadcasted_iota(jnp.int32, (W, W), 0)
    limit = jnp.where(slot_w >= TXT, lengths[:, 1:2] + TXT, lengths[:, 0:1])
    valid = jnp.where(slot_w < limit, 1.0, 0.0)
    attn_total = terms[z].astype(F32) + reached(0, 0, True) + reached(1, 0, True)
    d_gate = jnp.tanh(attn_gate[...])
    d_attn = (d_gate * attn_total * valid).astype(BF16)

    wait_for(recv.at[S_QT2], qt.at[0, pl.ds(0, 15)])
    to_sibling(S_QT3, qt.at[core])

    wait_for(recv.at[S_KV], kvr.at[pl.ds(0, N - 1)])
    kv_f = kvr[...].astype(F32)
    keys = kv_f[:, :8].reshape(256, W).astype(BF16)
    values = kv_f[:, 8:].reshape(256, W).astype(BF16)
    q_scaled = qs_v[...]
    weighted = jnp.exp(nt(q_scaled, keys)) * allowed
    probs = weighted / jnp.sum(weighted, axis=1, keepdims=True)
    probs_low = probs.astype(BF16)

    d_probs = nt(d_attn, values)
    delta = jnp.sum(d_probs * probs, axis=1, keepdims=True)
    d_scores_f = probs * (d_probs - delta)
    d_q_scaled = nn(d_scores_f.astype(BF16), keys)
    query_unit = qu_v[...]
    grad = d_q_scaled * q_gain[...] * scale
    d_queries = qi_v[...] * (grad - query_unit * jnp.mean(grad * query_unit, axis=1, keepdims=True))
    dqa[z] = d_queries.astype(BF16)

    def pass_on(from_z, hops):
        remote(dqa.at[from_z], dqa.at[from_z], send.at[S_DQ], dq_recv.at[from_z],
               (dp, z_at(hops))).start()

    def arrived(from_z):
        remote(dqa.at[from_z], dqa.at[from_z], send.at[S_DQ], dq_recv.at[from_z],
               (dp, z_at(1))).wait_recv()

    for hops in (3, -3, 1, -1):
        pass_on(z, hops)

    attn_out[...] = (nn(probs_low, values) * valid).astype(BF16)
    d_scores = d_scores_f.astype(BF16).astype(F32).T.astype(BF16)
    probs_t = probs_low.astype(F32).T.astype(BF16)
    d_keys = nn(d_scores, q_scaled)
    query_part = jnp.sum(d_q_scaled * query_unit, axis=0, keepdims=True) * scale
    key_part = jnp.sum(
        d_keys.astype(BF16).astype(F32) * keys.astype(F32), axis=0, keepdims=True
    ) / k_gain[...]
    gs[...] = jnp.concatenate([query_part, key_part], axis=0)
    to_plane(S_G1, lambda to: gs, gr.at[dp])
    gr[dp] = gs[...]

    d_values = nn(probs_t, d_attn)
    kgs[...] = jnp.concatenate(
        [d_keys.reshape(N, 8, W), d_values.reshape(N, 8, W)], axis=1
    ).astype(BF16)
    seg = z // 8
    place = lax.rem(z, 8)

    def to_segment(n, _):
        to = lax.rem(place + n, 8)
        remote(kgs.at[pl.ds(4 * to, 4)], kg1.at[place], send.at[S_KG1], recv.at[S_KG1],
               (dp, 8 * seg + to)).start()
        return 0

    lax.fori_loop(1, 8, to_segment, 0)
    kg1[place] = kgs[pl.ds(4 * place, 4)]
    wait_for(recv.at[S_WG1], wg.at[pl.ds(0, 15), 0])
    to_sibling(S_WG2, wg.at[:, core])

    def text_term(head):
        return nt(dqa[head], qt[lax.rem(head, 2), head // 2])

    ways = ((1, 16), (-1, 15))

    def relay(m):
        for sign, most in ways:
            if 3 * m + 1 > most:
                continue
            near = z_at(-sign * (3 * m + 1))
            arrived(near)
            if 3 * m + 2 <= most:
                pass_on(near, sign)
        if m == 5:
            return
        for sign, most in ways:
            far = z_at(-sign * (3 * m + 3))
            arrived(far)
            if 3 * m + 6 <= most:
                pass_on(far, 3 * sign)
            if 3 * m + 4 <= most:
                pass_on(far, sign)

    def use(m):
        heads = []
        for j in (1, 3, 2):
            for sign, most in ways:
                if 3 * m + j <= most:
                    heads.append(z_at(-sign * (3 * m + j)))
                    if j == 2:
                        arrived(heads[-1])
        acc[...] = acc[...] + nt(
            jnp.concatenate([dqa[h] for h in heads], axis=1),
            jnp.concatenate([qt[lax.rem(h, 2), h // 2] for h in heads], axis=1),
        )

    relay(0)

    wait_for(recv.at[S_KG1], kg1.at[pl.ds(0, 7)])
    kg2[...] = jnp.sum(kg1[...].astype(F32), axis=0).astype(BF16)
    for j in range(4):
        to_owner = 4 * place + j

        @pl.when(to_owner != z)
        def _():
            remote(kg2.at[j], kgr.at[seg], send.at[S_KG2], recv.at[S_KG2], (dp, to_owner)).start()

        @pl.when(to_owner == z)
        def _():
            kgr[seg] = kg2[j]

    wait_for(recv.at[S_G1], gr.at[pl.ds(0, N - 1)])
    gs2[...] = jnp.sum(gr[...], axis=0)
    to_z(S_G2, lambda to: gs2, gr2.at[z])
    gr2[z] = gs2[...]

    wait_for(recv.at[S_QT3], qt.at[0])
    acc[...] = text_term(z)

    relay(1)
    use(0)
    relay(2)
    use(1)
    relay(3)
    use(2)
    relay(4)
    use(3)

    summing = 4 * place <= z
    summing = jnp.logical_and(summing, z < 4 * place + 4)

    @pl.when(summing)
    def _():
        wait_for(recv.at[S_KG2], kgr.at[pl.ds(0, 3)])

    @pl.when(jnp.logical_not(summing))
    def _():
        wait_for(recv.at[S_KG2], kgr)

    kv_sum = kgr[...].astype(F32)
    d_projected = []
    for k in range(4):
        key_unit = ku_v[k]
        key_grad = kv_sum[k, :8] * k_gain[...]
        d_projected.append(ki_v[k] * (
            key_grad - key_unit * jnp.mean(key_grad * key_unit, axis=1, keepdims=True)
        ))
        d_projected.append(kv_sum[k, 8:])
    wait_for(recv.at[S_WG2], wg.at[:, 0])
    d_normed = nn(
        jnp.concatenate(d_projected, axis=1).astype(BF16), wg[...].reshape(1024, ENC)
    )
    feat_grad = d_normed * jnp.concatenate([enc_gain[n : n + 1] for n in range(10)], axis=1)
    unit = unit_v[...]
    feat_out[...] = (
        istd_v[:, :1]
        * (
            feat_grad
            - jnp.mean(feat_grad, axis=1, keepdims=True)
            - unit * jnp.mean(feat_grad * unit, axis=1, keepdims=True)
        )
    ).astype(BF16)

    use(4)
    relay(5)
    use(5)
    text_out[...] = acc[...].astype(BF16)

    wait_for(recv.at[S_G2], gr2.at[pl.ds(0, N - 1)])
    gains = jnp.sum(gr2[...], axis=0)
    qg_out[...] = gains[0:1]
    kg_out[...] = gains[1:2]

    wait_for(send.at[S_C], terms.at[pl.ds(0, N - 1)])
    wait_for(send.at[S_NRM], nrm.at[pl.ds(0, N - 1)])
    wait_for(send.at[S_PLA], pp.at[pl.ds(0, N - 1)])
    wait_for(send.at[S_KV], kvr.at[pl.ds(0, N - 1)])
    wait_for(send.at[S_KG1], kg1.at[pl.ds(0, 7)])
    wait_for(send.at[S_G1], gr.at[pl.ds(0, N - 1)])
    wait_for(send.at[S_G2], gr2.at[pl.ds(0, N - 1)])
    wait_for(send.at[S_QT2], qt.at[0, pl.ds(0, 15)])
    wait_for(send.at[S_QT3], qt.at[0])
    wait_for(send.at[S_WG1], wg.at[pl.ds(0, 15), 0])
    wait_for(send.at[S_WG2], wg.at[:, 0])
    wait_for(send.at[S_DQ], dqa.at[pl.ds(0, N - 1)])

    @pl.when(summing)
    def _():
        wait_for(send.at[S_KG2], kgr.at[pl.ds(0, 3)])

    @pl.when(jnp.logical_not(summing))
    def _():
        wait_for(send.at[S_KG2], kgr)

    @pl.when(owning)
    def _():
        wait_for(send.at[S_WRS], wr.at[pl.ds(0, TILES - 1)])
        wait_for(send.at[S_WAG], wr.at[pl.ds(0, N - 1)])

    @pl.when(jnp.logical_not(owning))
    def _():
        wait_for(send.at[S_WRS], wr.at[pl.ds(0, TILES)])

    @pl.when(even)
    def _():
        wait_for(send.at[S_QT1], kvr.at[pl.ds(0, N - 1)])


def on_device(
    text, q_weight, q_gain, enc_hidden, enc_branch, enc_gate, enc_gain, enc_bias,
    proj_weight, proj_bias, kv_weight, k_gain, attn_gate, o_weight, d_update,
    tile_counts, image_sample, text_lengths,
):
    vmem = pl.BlockSpec(memory_space=pltpu.VMEM)
    anywhere = pl.BlockSpec(memory_space=pl.ANY)
    arguments = (
        enc_hidden, enc_branch, enc_gate.reshape(1, 1), enc_gain.reshape(10, W),
        enc_bias.reshape(10, W), proj_weight, kv_weight, proj_bias.reshape(1, 256),
        d_update, o_weight, tile_counts, image_sample, text_lengths, attn_gate.reshape(1, 1),
        q_gain.reshape(1, W), k_gain.reshape(1, W), q_weight, text,
    )
    scratch = [pltpu.VMEM(a.shape, a.dtype) for a in arguments] + [
        pltpu.VMEM((N, 16, HALF), BF16),
        pltpu.VMEM((W, AUG), BF16),
        pltpu.VMEM((N, 16, W), BF16),
        pltpu.VMEM((16, W), BF16),
        pltpu.VMEM((W, AUG), BF16),
        pltpu.VMEM((16, 2, 32, ENC), BF16),
        pltpu.VMEM((N, 8, W), F32), pltpu.VMEM((N, 8, W), F32),
        pltpu.VMEM((4, 16, W), BF16), pltpu.VMEM((N, 16, W), BF16),
        pltpu.VMEM((N, 16, W), BF16), pltpu.VMEM((8, 4, 16, W), BF16),
        pltpu.VMEM((4, 16, W), BF16), pltpu.VMEM((4, 16, W), BF16),
        pltpu.VMEM((2, W), F32), pltpu.VMEM((N, 2, W), F32),
        pltpu.VMEM((2, W), F32), pltpu.VMEM((N, 2, W), F32),
        pltpu.VMEM((N, W, W), BF16),
        pltpu.VMEM((2, 8, W, W), BF16), pltpu.VMEM((2, 8, W, W), BF16),
        pltpu.VMEM((N, W, W), BF16),
        pltpu.VMEM((2, 16, 256, W), BF16),
        pltpu.VMEM((W, W), F32), pltpu.VMEM((W, W), BF16), pltpu.VMEM((W, W), F32),
        pltpu.VMEM((4, 8, W), F32), pltpu.VMEM((4, 8, W), F32),
        pltpu.VMEM((8, ENC), F32), pltpu.VMEM((8, W), F32),
        pltpu.VMEM((W, 256), F32),
        pltpu.SemaphoreType.DMA((len(arguments),)),
        pltpu.SemaphoreType.DMA((16,)), pltpu.SemaphoreType.DMA((16,)),
        pltpu.SemaphoreType.DMA((2, 8)), pltpu.SemaphoreType.DMA((2, 8)),
        pltpu.SemaphoreType.DMA((N,)),
    ]
    attn, d_text, d_features, d_q_gain, d_k_gain = pl.pallas_call(
        kernel,
        out_shape=(
            jax.ShapeDtypeStruct((128, W), BF16),
            jax.ShapeDtypeStruct((128, 256), BF16),
            jax.ShapeDtypeStruct((8, ENC), BF16),
            jax.ShapeDtypeStruct((1, W), F32),
            jax.ShapeDtypeStruct((1, W), F32),
        ),
        in_specs=[anywhere] * len(arguments),
        out_specs=(vmem,) * 5,
        scratch_shapes=scratch,
        compiler_params=pltpu.CompilerParams(
            collective_id=0, has_side_effects=True, vmem_limit_bytes=60 << 20
        ),
        name="layer",
    )(*arguments)
    return attn, d_text, d_features, d_q_gain.reshape(W), d_k_gain.reshape(W)


def solution(mesh):
    in_specs = (
        P("dp", None),
        P(None, "head"),
        P(),
        P(("dp", "head"), None),
        P(("dp", "head"), None),
        P(),
        P(),
        P(),
        P(None, "head"),
        P("head"),
        P("head", None),
        P(),
        P(),
        P(None, "head"),
        P("dp", "head"),
        P("dp", None),
        P("dp", None),
        P("dp", None),
    )
    out_specs = (P("dp", "head"), P("dp", "head"), P(("dp", "head"), None), P(), P())
    return jax.shard_map(
        on_device, mesh=mesh, in_specs=in_specs, out_specs=out_specs, check_vma=False
    )
```

```python
import jax
import jax.numpy as jnp
from jax import lax
from jax.experimental import pallas as pl
from jax.experimental.pallas import tpu as pltpu
from jax.sharding import PartitionSpec as P

N = 32
TXT = 64
TILE = 32
W = 128
ENC = 1280
HALF = 640
AUG = 1408
TILES = 22
EPSILON = 1e-05
MESH = pl.DeviceIdType.MESH
F32 = jnp.float32
BF16 = jnp.bfloat16

(
    S_NRM, S_WRS, S_WAG, S_PLA, S_KV, S_KG1, S_KG2, S_G1, S_G2, S_QT1, S_QT2, S_QT3, S_WG1, S_WG2, S_DQ, S_C,
) = range(16)


def nn(a, b):
    return lax.dot_general(a, b, (((1,), (0,)), ((), ())), preferred_element_type=F32)


def nt(a, b):
    return lax.dot_general(a, b, (((1,), (1,)), ((), ())), preferred_element_type=F32)


def tn(a, b):
    return lax.dot_general(a, b, (((0,), (0,)), ((), ())), preferred_element_type=F32)


def kernel(
    enc_hidden_h, enc_branch_h, enc_gate_h, enc_gain_h, enc_bias_h, proj_weight, kv_weight, proj_bias_h,
    d_update_h, o_weight, tiles_h, owners_h, lengths_h, attn_gate_h, q_gain_h, k_gain_h,
    q_weight, text,
    attn_out, text_out, feat_out, qg_out, kg_out,
    enc_hidden, enc_branch, enc_gate, enc_gain, enc_bias, pw_v, kvw_v, proj_bias,
    d_update, ow_v, tiles, owners, lengths, attn_gate, q_gain, k_gain, qw_v, text_v,
    nrm, wt, wr, ws, wf, wg, pp, pr, kvs, kvr, kgs, kg1, kg2, kgr,
    gs, gr, gs2, gr2, terms, rx1, rx2, dqa, qt,
    qu_v, qs_v, qi_v, ku_v, ki_v, unit_v, istd_v, acc,
    load_sem, send, recv, c1_recv, c2_recv, dq_recv,
):
    dp = lax.axis_index("dp")
    z = lax.axis_index("head")

    def z_at(k):
        return lax.rem(z + k + 2 * N, N)

    def remote(src, dst, s_sem, r_sem, dev):
        return pltpu.make_async_remote_copy(
            src_ref=src, dst_ref=dst, send_sem=s_sem, recv_sem=r_sem,
            device_id=dev, device_id_type=MESH,
        )

    def wait_for(sem, ref):
        pltpu.make_async_copy(ref, ref, sem).wait()

    def far_first(n):
        step = (n + 1) // 2
        return jnp.where(lax.rem(n, 2) == 1, 16 + step, 16 - step)

    def to_z(stage, src_of, dst):
        def one(n, _):
            to = z_at(far_first(n))
            remote(src_of(to), dst, send.at[stage], recv.at[stage], (dp, to)).start()
            return 0
        lax.fori_loop(0, N - 1, one, 0)

    def to_plane(stage, src_of, dst):
        def one(n, _):
            to = lax.rem(dp + far_first(n), N)
            remote(src_of(to), dst, send.at[stage], recv.at[stage], (to, z)).start()
            return 0
        lax.fori_loop(0, N - 1, one, 0)

    loads = [
        pltpu.make_async_copy(src, dst, load_sem.at[n])
        for n, (src, dst) in enumerate((
            (kv_weight, kvw_v), (proj_weight, pw_v), (proj_bias_h, proj_bias),
            (enc_hidden_h, enc_hidden), (enc_branch_h, enc_branch), (enc_gate_h, enc_gate),
            (enc_gain_h, enc_gain), (enc_bias_h, enc_bias), (d_update_h, d_update),
            (o_weight, ow_v), (tiles_h, tiles), (owners_h, owners), (lengths_h, lengths),
            (attn_gate_h, attn_gate), (q_gain_h, q_gain), (k_gain_h, k_gain),
            (q_weight, qw_v), (text, text_v),
        ))
    ]
    for load in loads:
        load.start()
    wf[...] = jnp.zeros_like(wf)

    barrier = pltpu.get_barrier_semaphore()

    def greet(k, _):
        pl.semaphore_signal(barrier, inc=1, device_id=(dp, z_at(k)), device_id_type=MESH)
        pl.semaphore_signal(
            barrier, inc=1, device_id=(lax.rem(dp + k, N), z), device_id_type=MESH
        )
        return 0

    lax.fori_loop(1, N, greet, 0)

    block = dp // 4
    quarter = lax.rem(dp, 4)
    rows0 = 32 * quarter
    for load in loads[:3]:
        load.wait()
    kv_t = kvw_v[:, pl.ds(pl.multiple_of(W * block, W), W)].astype(F32).T.astype(BF16)
    wt[:, :ENC] = nt(kv_t, pw_v[...]).astype(BF16)
    first_row = lax.broadcasted_iota(jnp.int32, (W, 256), 0) == 0
    bias_rows = jnp.where(first_row, jnp.broadcast_to(proj_bias[...], (W, 256)), 0.0).astype(BF16)
    wt[:, ENC:] = nt(kv_t, bias_rows).astype(BF16)

    def tile_of(ref, t):
        row = pl.multiple_of(rows0 + 16 * (t // 11), 16)
        col = pl.multiple_of(W * lax.rem(t, 11), W)
        return ref.at[pl.ds(row, 16), pl.ds(col, W)]

    own_tile = (11 * z + 15) // 16
    owning = jnp.logical_and(own_tile < TILES, (16 * own_tile) // 11 == z)

    pl.semaphore_wait(barrier, 2 * (N - 1))

    def send_tile(n, _):
        t = lax.rem((11 * z_at(16) + 15) // 16 + n, TILES)
        to = (16 * t) // 11

        @pl.when(to != z)
        def _():
            remote(tile_of(wt, t), wr.at[z], send.at[S_WRS], recv.at[S_WRS], (dp, to)).start()
        return 0

    lax.fori_loop(0, TILES, send_tile, 0)

    for load in loads[8:10]:
        load.wait()
    for n in range(4):
        heads = nt(d_update[...], ow_v[1024 * n : 1024 * (n + 1)]).astype(BF16)
        for j in range(8):
            terms[8 * n + j] = heads[:, W * j : W * (j + 1)]

    sides = ((0, 1), (1, -1))

    def odd_terms(high, low):
        def one(n, _):
            j = high - n
            for side, sign in sides:
                remote(terms.at[z_at(sign * (2 * j + 1))], rx1.at[side, j], send.at[S_C],
                       c1_recv.at[side, j], (dp, z_at(sign))).start()
            return 0
        lax.fori_loop(0, high - low + 1, one, 0)

    def reached(side, j, long):
        remote(terms.at[z], rx1.at[side, j], send.at[S_C], c1_recv.at[side, j],
               (dp, z_at(1))).wait_recv()
        total = rx1[side, j].astype(F32)
        if long:
            remote(terms.at[z], rx2.at[side, j], send.at[S_C], c2_recv.at[side, j],
                   (dp, z_at(1))).wait_recv()
            total = total + rx2[side, j].astype(F32)
        return total

    def send_on(side, sign, j, long):
        at = z_at(sign * 2 * j)
        terms[at] = (terms[at].astype(F32) + reached(side, j, long)).astype(BF16)
        remote(terms.at[at], rx2.at[side, j - 1], send.at[S_C], c2_recv.at[side, j - 1],
               (dp, z_at(2 * sign))).start()

    def next_terms(high, low):
        def one(n, _):
            for side, sign in sides:
                send_on(side, sign, high - n, True)
            return 0
        lax.fori_loop(0, high - low + 1, one, 0)

    chip = dp // 2
    core = lax.rem(dp, 2)

    def to_chips(stage, src, dst):
        def one(n, _):
            to = lax.rem(dp + 2 * n, N)
            remote(src, dst, send.at[stage], recv.at[stage], (to, z)).start()
            return 0
        lax.fori_loop(1, 16, one, 0)

    def to_sibling(stage, ref):
        remote(ref, ref, send.at[stage], recv.at[stage], (dp + 1 - 2 * core, z)).start()

    remote(terms.at[z_at(16)], rx2.at[0, 7], send.at[S_C], c2_recv.at[0, 7], (dp, z_at(2))).start()
    odd_terms(7, 5)

    for load in loads[3:8]:
        load.wait()
    gate = jnp.tanh(enc_gate[...])
    gain_row = jnp.concatenate([enc_gain[n : n + 1] for n in range(10)], axis=1)
    bias_row = jnp.concatenate([enc_bias[n : n + 1] for n in range(10)], axis=1)
    features = enc_hidden[...].astype(F32) + gate * enc_branch[...].astype(F32)
    centered = features - jnp.mean(features, axis=1, keepdims=True)
    inv_std = lax.rsqrt(jnp.mean(centered * centered, axis=1, keepdims=True) + EPSILON)
    unit = centered * inv_std
    unit_v[...] = unit
    istd_v[...] = jnp.broadcast_to(inv_std, (8, W))
    normed = unit * gain_row + bias_row
    nrm[dp] = jnp.concatenate([normed[:, :HALF], normed[:, HALF:]], axis=0).astype(BF16)

    to_plane(S_NRM, lambda to: nrm.at[dp], nrm.at[dp])

    for load in loads[10:]:
        load.wait()
    query_pre = nn(text_v[...], qw_v[...])
    inv_query = lax.rsqrt(jnp.mean(query_pre * query_pre, axis=1, keepdims=True) + EPSILON)
    scale = W ** (-0.5)
    query_unit = query_pre * inv_query
    qu_v[...] = query_unit
    qi_v[...] = jnp.broadcast_to(inv_query, (W, W))
    qs_v[...] = (query_unit * q_gain[...] * scale).astype(BF16)


    @pl.when(owning)
    def _():
        wait_for(recv.at[S_WRS], wr.at[pl.ds(0, N - 1)])
        wr[z] = tile_of(wt, own_tile)[...]
        tile = jnp.sum(wr[...].astype(F32), axis=0).astype(BF16)
        ws[...] = tile
        tile_of(wf, own_tile)[...] = tile
        to_z(S_WAG, lambda to: ws, tile_of(wf, own_tile))

    odd_terms(4, 3)
    send_on(1, -1, 7, False)
    send_on(0, 1, 7, True)
    next_terms(6, 5)

    @pl.when(owning)
    def _():
        wait_for(recv.at[S_WAG], wr.at[pl.ds(0, TILES - 1)])

    @pl.when(jnp.logical_not(owning))
    def _():
        wait_for(recv.at[S_WAG], wr.at[pl.ds(0, TILES)])

    wait_for(recv.at[S_NRM], nrm.at[pl.ds(0, N - 1)])

    plane = nrm[...].reshape(2 * 256, HALF)
    half_a = nt(plane, wf[:, :HALF]).reshape(N, 16, W)
    half_b = nt(plane, wf[:, HALF:ENC]).reshape(N, 16, W)
    ones = jnp.where(lax.broadcasted_iota(jnp.int32, (8, W), 1) == 0, 1.0, 0.0).astype(BF16)
    bias = nt(ones, wf[:, ENC:])
    pp[...] = half_a[:, :8] + half_b[:, 8:] + bias[None]
    to_plane(S_PLA, lambda to: pp.at[to], pr.at[dp])
    pr[dp] = pp[dp]

    own_rows = wf.at[pl.ds(pl.multiple_of(rows0, 32), 32), pl.ds(0, ENC)]
    wg[chip, core] = own_rows[...]

    odd_terms(2, 0)
    part = pl.ds(pl.multiple_of(16 * chip, 16), 16)
    even = lax.rem(z, 2) == core

    @pl.when(even)
    def _():
        to_z(
            S_QT1,
            lambda to: qw_v.at[pl.ds(pl.multiple_of(256 * to + 16 * chip, 16), 16)],
            qt.at[core, z // 2, part],
        )
        qt[core, z // 2, part] = qw_v[pl.ds(pl.multiple_of(256 * z + 16 * chip, 16), 16)]

    next_terms(4, 3)

    wait_for(recv.at[S_PLA], pr.at[pl.ds(0, N - 1)])
    blocks = jnp.sum(pr[...].reshape(8, 4, 8, W), axis=1)
    for k in range(4):
        key_pre = blocks[2 * k]
        inv_key = lax.rsqrt(jnp.mean(key_pre * key_pre, axis=1, keepdims=True) + EPSILON)
        key_unit = key_pre * inv_key
        ku_v[k] = key_unit
        ki_v[k] = jnp.broadcast_to(inv_key, (8, W))
        kvs[k] = jnp.concatenate([key_unit * k_gain[...], blocks[2 * k + 1]], axis=0).astype(BF16)
    to_z(S_KV, lambda to: kvs.at[to // 8], kvr.at[z])
    kvr[z] = kvs[z // 8]
    to_chips(S_WG1, wg.at[chip, core], wg.at[chip, core])

    @pl.when(even)
    def _():
        wait_for(recv.at[S_QT1], kvr.at[pl.ds(0, 15)])

    @pl.when(jnp.logical_not(even))
    def _():
        wait_for(recv.at[S_QT1], kvr.at[pl.ds(0, 16)])

    to_chips(S_QT2, qt.at[core, :, part], qt.at[core, :, part])


    next_terms(2, 1)

    row = lax.broadcasted_iota(jnp.int32, (W, 256), 1)
    slot = lax.broadcasted_iota(jnp.int32, (W, 256), 0)
    end0 = tiles[:, 0:1] * TILE
    end1 = end0 + tiles[:, 1:2] * TILE
    key_sample = jnp.where(
        row < end0, owners[:, 0:1], jnp.where(row < end1, owners[:, 1:2], owners[:, 2:3])
    )
    allowed = jnp.where((slot >= TXT).astype(jnp.int32) == key_sample, 1.0, 0.0)
    slot_w = lax.broadcasted_iota(jnp.int32, (W, W), 0)
    limit = jnp.where(slot_w >= TXT, lengths[:, 1:2] + TXT, lengths[:, 0:1])
    valid = jnp.where(slot_w < limit, 1.0, 0.0)
    attn_total = terms[z].astype(F32) + reached(0, 0, True) + reached(1, 0, True)
    d_gate = jnp.tanh(attn_gate[...])
    d_attn = (d_gate * attn_total * valid).astype(BF16)

    wait_for(recv.at[S_KV], kvr.at[pl.ds(0, N - 1)])
    kv_f = kvr[...].astype(F32)
    keys = kv_f[:, :8].reshape(256, W).astype(BF16)
    values = kv_f[:, 8:].reshape(256, W).astype(BF16)
    q_scaled = qs_v[...]
    weighted = jnp.exp(nt(q_scaled, keys)) * allowed
    probs = weighted / jnp.sum(weighted, axis=1, keepdims=True)
    probs_low = probs.astype(BF16)

    d_probs = nt(d_attn, values)
    delta = jnp.sum(d_probs * probs, axis=1, keepdims=True)
    d_scores_f = probs * (d_probs - delta)
    d_q_scaled = nn(d_scores_f.astype(BF16), keys)
    query_unit = qu_v[...]
    grad = d_q_scaled * q_gain[...] * scale
    d_queries = qi_v[...] * (grad - query_unit * jnp.mean(grad * query_unit, axis=1, keepdims=True))
    dqa[z] = d_queries.astype(BF16)

    def pass_on(from_z, hops):
        remote(dqa.at[from_z], dqa.at[from_z], send.at[S_DQ], dq_recv.at[from_z],
               (dp, z_at(hops))).start()

    def arrived(from_z):
        remote(dqa.at[from_z], dqa.at[from_z], send.at[S_DQ], dq_recv.at[from_z],
               (dp, z_at(1))).wait_recv()

    def text_term(head):
        return nt(dqa[head], qt[lax.rem(head, 2), head // 2])

    ways = ((1, 16), (-1, 15))

    def relay(m):
        for sign, most in ways:
            if 3 * m + 1 > most:
                continue
            near = z_at(-sign * (3 * m + 1))
            arrived(near)
            if 3 * m + 2 <= most:
                pass_on(near, sign)
        if m == 5:
            return
        for sign, most in ways:
            far = z_at(-sign * (3 * m + 3))
            arrived(far)
            if 3 * m + 6 <= most:
                pass_on(far, 3 * sign)
            if 3 * m + 4 <= most:
                pass_on(far, sign)

    def use(m):
        heads = []
        for j in (1, 3, 2):
            for sign, most in ways:
                if 3 * m + j <= most:
                    heads.append(z_at(-sign * (3 * m + j)))
                    if j == 2:
                        arrived(heads[-1])
        acc[...] = acc[...] + nt(
            jnp.concatenate([dqa[h] for h in heads], axis=1),
            jnp.concatenate([qt[lax.rem(h, 2), h // 2] for h in heads], axis=1),
        )

    for hops in (3, -3, 1, -1):
        pass_on(z, hops)

    d_scores = d_scores_f.astype(BF16).astype(F32).T.astype(BF16)
    d_keys = nn(d_scores, q_scaled)
    query_part = jnp.sum(d_q_scaled * query_unit, axis=0, keepdims=True) * scale
    key_part = jnp.sum(
        d_keys.astype(BF16).astype(F32) * keys.astype(F32), axis=0, keepdims=True
    ) / k_gain[...]
    gs[...] = jnp.concatenate([query_part, key_part], axis=0)
    to_plane(S_G1, lambda to: gs, gr.at[dp])
    gr[dp] = gs[...]

    relay(0)

    probs_t = probs_low.astype(F32).T.astype(BF16)
    d_values = nn(probs_t, d_attn)
    kgs[...] = jnp.concatenate(
        [d_keys.reshape(N, 8, W), d_values.reshape(N, 8, W)], axis=1
    ).astype(BF16)
    seg = z // 8
    place = lax.rem(z, 8)

    def to_segment(n, _):
        to = lax.rem(place + n, 8)
        remote(kgs.at[pl.ds(4 * to, 4)], kg1.at[place], send.at[S_KG1], recv.at[S_KG1],
               (dp, 8 * seg + to)).start()
        return 0

    lax.fori_loop(1, 8, to_segment, 0)
    kg1[place] = kgs[pl.ds(4 * place, 4)]

    relay(1)

    wait_for(recv.at[S_G1], gr.at[pl.ds(0, N - 1)])
    gs2[...] = jnp.sum(gr[...], axis=0)
    to_z(S_G2, lambda to: gs2, gr2.at[z])
    gr2[z] = gs2[...]

    relay(2)

    wait_for(recv.at[S_QT2], qt.at[0, pl.ds(0, 15)])
    to_sibling(S_QT3, qt.at[core])

    wait_for(recv.at[S_KG1], kg1.at[pl.ds(0, 7)])
    kg2[...] = jnp.sum(kg1[...].astype(F32), axis=0).astype(BF16)
    for j in range(4):
        to_owner = 4 * place + j

        @pl.when(to_owner != z)
        def _():
            remote(kg2.at[j], kgr.at[seg], send.at[S_KG2], recv.at[S_KG2], (dp, to_owner)).start()

        @pl.when(to_owner == z)
        def _():
            kgr[seg] = kg2[j]

    wait_for(recv.at[S_WG1], wg.at[pl.ds(0, 15), 0])
    to_sibling(S_WG2, wg.at[:, core])
    attn_out[...] = (nn(probs_low, values) * valid).astype(BF16)

    wait_for(recv.at[S_QT3], qt.at[0])
    acc[...] = text_term(z)
    use(0)

    relay(3)
    use(1)
    use(2)
    relay(4)
    use(3)

    summing = 4 * place <= z
    summing = jnp.logical_and(summing, z < 4 * place + 4)

    @pl.when(summing)
    def _():
        wait_for(recv.at[S_KG2], kgr.at[pl.ds(0, 3)])

    @pl.when(jnp.logical_not(summing))
    def _():
        wait_for(recv.at[S_KG2], kgr)

    kv_sum = kgr[...].astype(F32)
    d_projected = []
    for k in range(4):
        key_unit = ku_v[k]
        key_grad = kv_sum[k, :8] * k_gain[...]
        d_projected.append(ki_v[k] * (
            key_grad - key_unit * jnp.mean(key_grad * key_unit, axis=1, keepdims=True)
        ))
        d_projected.append(kv_sum[k, 8:])
    wait_for(recv.at[S_WG2], wg.at[:, 0])
    d_normed = nn(
        jnp.concatenate(d_projected, axis=1).astype(BF16), wg[...].reshape(1024, ENC)
    )
    feat_grad = d_normed * jnp.concatenate([enc_gain[n : n + 1] for n in range(10)], axis=1)
    unit = unit_v[...]
    feat_out[...] = (
        istd_v[:, :1]
        * (
            feat_grad
            - jnp.mean(feat_grad, axis=1, keepdims=True)
            - unit * jnp.mean(feat_grad * unit, axis=1, keepdims=True)
        )
    ).astype(BF16)

    use(4)
    relay(5)
    use(5)
    text_out[...] = acc[...].astype(BF16)

    wait_for(recv.at[S_G2], gr2.at[pl.ds(0, N - 1)])
    gains = jnp.sum(gr2[...], axis=0)
    qg_out[...] = gains[0:1]
    kg_out[...] = gains[1:2]

    wait_for(send.at[S_C], terms.at[pl.ds(0, N - 1)])
    wait_for(send.at[S_NRM], nrm.at[pl.ds(0, N - 1)])
    wait_for(send.at[S_PLA], pp.at[pl.ds(0, N - 1)])
    wait_for(send.at[S_KV], kvr.at[pl.ds(0, N - 1)])
    wait_for(send.at[S_KG1], kg1.at[pl.ds(0, 7)])
    wait_for(send.at[S_G1], gr.at[pl.ds(0, N - 1)])
    wait_for(send.at[S_G2], gr2.at[pl.ds(0, N - 1)])
    wait_for(send.at[S_QT2], qt.at[0, pl.ds(0, 15)])
    wait_for(send.at[S_QT3], qt.at[0])
    wait_for(send.at[S_WG1], wg.at[pl.ds(0, 15), 0])
    wait_for(send.at[S_WG2], wg.at[:, 0])
    wait_for(send.at[S_DQ], dqa.at[pl.ds(0, N - 1)])

    @pl.when(summing)
    def _():
        wait_for(send.at[S_KG2], kgr.at[pl.ds(0, 3)])

    @pl.when(jnp.logical_not(summing))
    def _():
        wait_for(send.at[S_KG2], kgr)

    @pl.when(owning)
    def _():
        wait_for(send.at[S_WRS], wr.at[pl.ds(0, TILES - 1)])
        wait_for(send.at[S_WAG], wr.at[pl.ds(0, N - 1)])

    @pl.when(jnp.logical_not(owning))
    def _():
        wait_for(send.at[S_WRS], wr.at[pl.ds(0, TILES)])

    @pl.when(even)
    def _():
        wait_for(send.at[S_QT1], kvr.at[pl.ds(0, N - 1)])


def hand_over(*refs):
    sems = refs[15]
    loads = [pltpu.make_async_copy(refs[n], refs[10 + n], sems.at[n]) for n in range(5)]
    stores = [pltpu.make_async_copy(refs[10 + n], refs[5 + n], sems.at[5 + n]) for n in range(5)]
    for load in loads:
        load.start()
    for load, store in zip(loads, stores):
        load.wait()
        store.start()
    for store in stores:
        store.wait()


def on_device(
    text, q_weight, q_gain, enc_hidden, enc_branch, enc_gate, enc_gain, enc_bias,
    proj_weight, proj_bias, kv_weight, k_gain, attn_gate, o_weight, d_update,
    tile_counts, image_sample, text_lengths,
):
    vmem = pl.BlockSpec(memory_space=pltpu.VMEM)
    anywhere = pl.BlockSpec(memory_space=pl.ANY)
    arguments = (
        enc_hidden, enc_branch, enc_gate.reshape(1, 1), enc_gain.reshape(10, W),
        enc_bias.reshape(10, W), proj_weight, kv_weight, proj_bias.reshape(1, 256),
        d_update, o_weight, tile_counts, image_sample, text_lengths, attn_gate.reshape(1, 1),
        q_gain.reshape(1, W), k_gain.reshape(1, W), q_weight, text,
    )
    scratch = [pltpu.VMEM(a.shape, a.dtype) for a in arguments] + [
        pltpu.VMEM((N, 16, HALF), BF16),
        pltpu.VMEM((W, AUG), BF16),
        pltpu.VMEM((N, 16, W), BF16),
        pltpu.VMEM((16, W), BF16),
        pltpu.VMEM((W, AUG), BF16),
        pltpu.VMEM((16, 2, 32, ENC), BF16),
        pltpu.VMEM((N, 8, W), F32), pltpu.VMEM((N, 8, W), F32),
        pltpu.VMEM((4, 16, W), BF16), pltpu.VMEM((N, 16, W), BF16),
        pltpu.VMEM((N, 16, W), BF16), pltpu.VMEM((8, 4, 16, W), BF16),
        pltpu.VMEM((4, 16, W), BF16), pltpu.VMEM((4, 16, W), BF16),
        pltpu.VMEM((2, W), F32), pltpu.VMEM((N, 2, W), F32),
        pltpu.VMEM((2, W), F32), pltpu.VMEM((N, 2, W), F32),
        pltpu.VMEM((N, W, W), BF16),
        pltpu.VMEM((2, 8, W, W), BF16), pltpu.VMEM((2, 8, W, W), BF16),
        pltpu.VMEM((N, W, W), BF16),
        pltpu.VMEM((2, 16, 256, W), BF16),
        pltpu.VMEM((W, W), F32), pltpu.VMEM((W, W), BF16), pltpu.VMEM((W, W), F32),
        pltpu.VMEM((4, 8, W), F32), pltpu.VMEM((4, 8, W), F32),
        pltpu.VMEM((8, ENC), F32), pltpu.VMEM((8, W), F32),
        pltpu.VMEM((W, 256), F32),
        pltpu.SemaphoreType.DMA((len(arguments),)),
        pltpu.SemaphoreType.DMA((16,)), pltpu.SemaphoreType.DMA((16,)),
        pltpu.SemaphoreType.DMA((2, 8)), pltpu.SemaphoreType.DMA((2, 8)),
        pltpu.SemaphoreType.DMA((N,)),
    ]
    results = pl.pallas_call(
        kernel,
        out_shape=(
            jax.ShapeDtypeStruct((128, W), BF16),
            jax.ShapeDtypeStruct((128, 256), BF16),
            jax.ShapeDtypeStruct((8, ENC), BF16),
            jax.ShapeDtypeStruct((1, W), F32),
            jax.ShapeDtypeStruct((1, W), F32),
        ),
        in_specs=[anywhere] * len(arguments),
        out_specs=(vmem,) * 5,
        scratch_shapes=scratch,
        compiler_params=pltpu.CompilerParams(
            collective_id=0, has_side_effects=True, vmem_limit_bytes=60 << 20
        ),
        name="layer",
    )(*arguments)
    attn, d_text, d_features, d_q_gain, d_k_gain = pl.pallas_call(
        hand_over,
        out_shape=tuple(jax.ShapeDtypeStruct(r.shape, r.dtype) for r in results),
        in_specs=[anywhere] * 5,
        out_specs=(anywhere,) * 5,
        scratch_shapes=[pltpu.VMEM(r.shape, r.dtype) for r in results]
        + [pltpu.SemaphoreType.DMA((10,))],
        compiler_params=pltpu.CompilerParams(vmem_limit_bytes=60 << 20),
        name="hand_over",
    )(*results)
    return attn, d_text, d_features, d_q_gain.reshape(W), d_k_gain.reshape(W)


def solution(mesh):
    in_specs = (
        P("dp", None),
        P(None, "head"),
        P(),
        P(("dp", "head"), None),
        P(("dp", "head"), None),
        P(),
        P(),
        P(),
        P(None, "head"),
        P("head"),
        P("head", None),
        P(),
        P(),
        P(None, "head"),
        P("dp", "head"),
        P("dp", None),
        P("dp", None),
        P("dp", None),
    )
    out_specs = (P("dp", "head"), P("dp", "head"), P(("dp", "head"), None), P(), P())
    return jax.shard_map(
        on_device, mesh=mesh, in_specs=in_specs, out_specs=out_specs, check_vma=False
    )
```
